256 devices in a mesh: dp: 4 (over y), row: 8 (over z), col: 8 (over x, core).
Axes of the slice: x: 4, y: 4, z: 8, core: 2. Of those that a mesh axis runs over, the one named last changes fastest.
Arguments:
- activations: bfloat16 [1024, 16384], P(('dp', 'col'), 'row'), may hold values from -6 to 6
- w_gate: bfloat16 [16384, 28672], P('row', ('dp', 'col')), may hold values from -0.046875 to 0.046875
- w_up: bfloat16 [16384, 28672], P('row', ('dp', 'col')), may hold values from -0.046875 to 0.046875
- w_down: bfloat16 [28672, 16384], P(('dp', 'col'), 'row'), may hold values from -0.03125 to 0.03125
- seq_lengths: int32 [4, 2], P('dp'), may hold values from 1 to 128
Outputs:
- block_out: bfloat16 [1024, 16384], P(('dp', 'col'), 'row')
The draws below stay inside these ranges and needn't reach their ends.
All inputs are finite; a program needn't handle non-finite values.
Results may differ from the reference program's by a relative error of at most 0.0049.
Values may be sent and summed in bfloat16 or wider, within the bound.
A program may use at most 128 MiB of HBM per device.

```python
import jax
import jax.numpy as jnp

D = 16384
FF = 28672
TOK_DEV = 32
SEQS = 2
TOKENS = 1024
SLOT = 128
N_DP = 4
N_COL = 8


def with_ends(values, key, low, largest):
    place = [jax.random.randint(jax.random.fold_in(key, axis), (), 0, length) for axis, length in enumerate(values.shape)]
    main_axis = values.shape.index(max(values.shape))
    next_to = place[:main_axis] + [(place[main_axis] + 1) % values.shape[main_axis]] + place[main_axis + 1:]
    return values.at[tuple(place)].set(low).at[tuple(next_to)].set(largest)


def block_scale(rng, shape, pieces, low, top_value):
    level, own = 1.0, jax.random.fold_in(rng, 6)
    for position, blocks in pieces:
        steps = jnp.exp(jax.random.uniform(jax.random.fold_in(own, position), (blocks,), jnp.float32, low / len(pieces), top_value / len(pieces)))
        level = level * jnp.repeat(steps, shape[position] // blocks).reshape([-1 if axis == position else 1 for axis in range(len(shape))])
    return level


def centred(key, shape, spread, limit, split=(), kind=jnp.bfloat16):
    drawn = spread * jax.random.normal(key, shape, jnp.float32)
    if split:
        drawn = drawn * block_scale(key, shape, split, -0.22, 0.18)
    return jnp.clip(drawn, -limit, limit).astype(kind)


def setup_inputs(seed: int = 0) -> dict:
    keys = jax.random.split(jax.random.key(seed), 6)
    activations = centred(keys[0], (TOKENS, D), 1.0, 6.0, ((0, 32), (1, 8)))
    w_gate = centred(keys[1], (D, FF), D ** -0.5, 0.046875, ((0, 8), (1, 32)))
    w_up = centred(keys[2], (D, FF), D ** -0.5, 0.046875, ((0, 8), (1, 32)))
    w_down = centred(keys[3], (FF, D), FF ** -0.5, 0.03125, ((0, 32), (1, 8)))
    seq_lengths = with_ends(jax.random.randint(keys[4], (N_DP, SEQS), 1, SLOT + 1), jax.random.fold_in(keys[4], 1), 1, SLOT).astype(jnp.int32)
    return dict(activations=activations, w_gate=w_gate, w_up=w_up, w_down=w_down, seq_lengths=seq_lengths)


def reference(activations, w_gate, w_up, w_down, seq_lengths):
    gate = jnp.dot(activations, w_gate, preferred_element_type=jnp.float32)
    up = jnp.dot(activations, w_up, preferred_element_type=jnp.float32)
    hidden = (jax.nn.silu(gate) * up).astype(jnp.bfloat16)
    projected = jnp.dot(hidden, w_down, preferred_element_type=jnp.float32)
    token_ids = jnp.arange(TOKENS, dtype=jnp.int32)
    group_size = TOK_DEV * N_COL
    groups = token_ids // group_size
    within = token_ids % group_size
    seq_index = within // SLOT
    offset = within % SLOT
    limits = seq_lengths[groups, seq_index]
    keep = (offset < limits).astype(jnp.float32)
    return (projected * keep[:, None]).astype(jnp.bfloat16)
```

```python
import jax
import jax.numpy as jnp
from jax import lax
from jax.experimental import pallas as pl
from jax.experimental.pallas import tpu as pltpu
from jax.sharding import PartitionSpec as P

MESH = pl.DeviceIdType.MESH
BF, F32 = jnp.bfloat16, jnp.float32
ROWS = 16
UNIT = 128
UNITS = [(0, 0), (1, 0), (3, 0), (2, 0), (1, 1), (2, 1), (3, 1), (0, 1)]
SUMS = ['two', 'chain', 'chain', 'chainf', 'chain', 'chain', 'chain', 'chain']
GATHERS = ['chain', 'chain', 'chain', 'chain', 'chain', 'chain', 'chain', 'chain']
ORDER = [
    ("x", 0), ("x", 1), ("bx", 0, 1), ("bx", 0, 3), ("bx", 0, 2), ("bx", 1, 1), ("bx", 1, 3), ("mm", 0, 0),
    ("mm", 0, 1), ("bx", 1, 2), ("mm", 7, 0), ("by", 1, 0), ("by", 3, 0), ("mm", 7, 1), ("mm", 1, 0),
    ("mm", 1, 1), ("r", 0, 1, 1), ("r", 0, 1, 0), ("mm", 2, 0), ("mm", 2, 1), ("r", 1, 1, 0), ("r", 1, 1, 1),
    ("by", 1, 1), ("by", 3, 1), ("r", 7, 1, 0), ("r", 7, 1, 1), ("mm", 4, 0), ("r", 2, 1, 1), ("g", 0),
    ("r", 2, 1, 0), ("by", 2, 0), ("r", 1, 2, 1), ("r", 1, 2, 0), ("mm", 4, 1), ("mm", 3, 0), ("r", 2, 2, 1),
    ("a", 0, 1, 0), ("a", 0, 1, 1), ("r", 4, 1, 0), ("mm", 3, 1), ("r", 1, 3, 1), ("r", 2, 2, 0), ("r", 1, 3, 0),
    ("r", 4, 1, 1), ("r", 3, 1, 0), ("by", 2, 1), ("r", 2, 3, 1), ("a", 0, 2, 0), ("a", 0, 2, 1), ("mm", 6, 0),
    ("mm", 5, 0), ("r", 2, 3, 0), ("r", 3, 1, 1), ("r", 4, 2, 0), ("mm", 5, 1), ("r", 4, 2, 1), ("g", 1),
    ("mm", 6, 1), ("a", 0, 3, 0), ("r", 6, 1, 0), ("a", 0, 3, 1), ("r", 3, 2, 1), ("r", 5, 1, 0), ("r", 3, 2, 0),
    ("r", 7, 2, 1), ("g", 2), ("r", 4, 3, 1), ("r", 5, 1, 1), ("a", 1, 1, 1), ("r", 4, 3, 0), ("r", 6, 1, 1),
    ("a", 1, 1, 0), ("pj", 0), ("r", 3, 3, 1), ("r", 6, 2, 0), ("r", 7, 2, 0), ("r", 7, 3, 1), ("r", 5, 2, 0),
    ("a", 2, 1, 1), ("sc", 0), ("r", 3, 3, 0), ("a", 2, 1, 0), ("r", 5, 2, 1), ("g", 4), ("a", 1, 2, 1),
    ("a", 1, 2, 0), ("r", 6, 2, 1), ("r", 6, 3, 0), ("r", 7, 3, 0), ("ty", 0), ("r", 5, 3, 0), ("a", 2, 2, 1),
    ("g", 3), ("r", 5, 3, 1), ("a", 2, 2, 0), ("a", 4, 1, 1), ("a", 4, 1, 0), ("a", 1, 3, 1), ("a", 1, 3, 0),
    ("r", 6, 3, 1), ("a", 2, 3, 1), ("a", 3, 1, 1), ("g", 7), ("g", 5), ("a", 4, 2, 1), ("a", 3, 1, 0),
    ("a", 2, 3, 0), ("a", 4, 2, 0), ("g", 6), ("pj", 1), ("a", 5, 1, 0), ("a", 7, 1, 1), ("a", 3, 2, 1),
    ("a", 3, 2, 0), ("a", 5, 1, 1), ("pj", 2), ("a", 4, 3, 0), ("sc", 1), ("a", 4, 3, 1), ("a", 5, 2, 0),
    ("a", 7, 2, 1), ("a", 6, 1, 1), ("a", 6, 1, 0), ("a", 3, 3, 0), ("a", 3, 3, 1), ("sc", 2), ("a", 5, 2, 1),
    ("a", 7, 1, 0), ("pj", 4), ("a", 7, 3, 1), ("a", 5, 3, 0), ("a", 6, 2, 1), ("a", 6, 2, 0), ("pj", 3),
    ("a", 5, 3, 1), ("a", 7, 2, 0), ("sc", 4), ("ty", 1), ("a", 6, 3, 1), ("a", 6, 3, 0), ("sc", 3), ("pj", 5),
    ("a", 7, 3, 0), ("ty", 2), ("pj", 6), ("sc", 5), ("pj", 7), ("ty", 4), ("sc", 6), ("ty", 3), ("sc", 7),
    ("ty", 5), ("ty", 6), ("ty", 7),
]
SLOT = {unit: i for i, unit in enumerate(UNITS)}
N = len(UNITS)
WIDE = [u for u in range(N) if SUMS[u] == "chainf"]
N_WIDE = max(1, len(WIDE))


def kernel(act, w_gate, w_up, w_down, lens, out, panel, wgu, wdn, part, rs_out, rs_in, wide_out, wide_in, hid, proj,
           swap_in, x_out, x_in, y_out, y_in, acc, w_sem, ax_s, ax_r, ak_s, ak_r, ay_s, ay_r, rs_s, rs_r, ag_s, ag_r,
           k_s, k_r, x_s, x_r, y_s, y_r):
    y, z, c = lax.axis_index("dp"), lax.axis_index("row"), lax.axis_index("col")
    x, k = c // 2, lax.rem(c, 2)
    ff = w_gate.shape[1]
    width = w_down.shape[1]
    half_cut = 512

    def at_x(step):
        return (y, z, 2 * lax.rem(x + step, 4) + k)

    def at_y(step):
        return (lax.rem(y + step, 4), z, c)

    def at_z(step):
        return (y, lax.rem(z + step + 8, 8), c)

    sibling = (y, z, 2 * x + 1 - k)
    peers = [at_x(1), at_x(2), at_x(3), at_y(1), at_y(2), at_y(3), at_z(1), at_z(-1), at_z(2), at_z(-2), sibling]
    sent, live = [], {}

    def send(name, src, dst, ss, rs, device):
        copy = pltpu.make_async_remote_copy(src_ref=src, dst_ref=dst, send_sem=ss, recv_sem=rs, device_id=device,
                                            device_id_type=MESH)
        copy.start()
        sent.append(copy)
        live[name] = copy

    def arrived(*name):
        live.pop(name).wait_recv()

    weights = [
        pltpu.make_async_copy(w_gate, wgu.at[:, 0:ff], w_sem.at[0]),
        pltpu.make_async_copy(w_up, wgu.at[:, ff:2 * ff], w_sem.at[1]),
        pltpu.make_async_copy(w_down, wdn, w_sem.at[2]),
    ]
    barrier = pltpu.get_barrier_semaphore()
    for peer in peers:
        pl.semaphore_signal(barrier, inc=1, device_id=peer, device_id_type=MESH)
    for copy in weights:
        copy.start()
    pl.semaphore_wait(barrier, len(peers))
    loaded = set()

    def load(i):
        if i not in loaded:
            loaded.add(i)
            weights[i].wait()

    def block(plane, place):
        return pl.ds(pl.multiple_of((plane * 4 + place) * ROWS, ROWS), ROWS)

    def plane(which):
        return pl.ds(pl.multiple_of(which * 4 * ROWS, 4 * ROWS), 4 * ROWS)

    def chunk(step):
        return pl.ds(pl.multiple_of(lax.rem(z + step + 8, 8) * ROWS, ROWS), ROWS)

    def to_column(half, i, src):
        place = lax.rem(x + 4 - i, 4)
        slot = SLOT[(0, half)]
        send(("sb", slot, i), src, panel.at[slot, block(k, place)], ak_s.at[slot, i], ak_r.at[slot, i], sibling)
        for step in (1, 3):
            there = SLOT[(4 - step, half)]
            send(("ay", there, i), src, panel.at[there, block(k, place)], ay_s.at[there, i], ay_r.at[there, i],
                 at_y(step))

    def op_x(half):
        rows = pl.ds(half * ROWS, ROWS)
        slot = SLOT[(0, half)]
        for step in (1, 3, 2):
            send(("ax", half, step), act.at[rows], panel.at[slot, block(k, x)], ax_s.at[half, step - 1],
                 ax_r.at[half, step - 1], at_x(step))
        to_column(half, 0, act.at[rows])
        panel[slot, block(k, x), :] = act[rows, :]

    def op_bx(half, i):
        arrived("ax", half, i)
        to_column(half, i, panel.at[SLOT[(0, half)], block(k, lax.rem(x + 4 - i, 4))])

    def op_by(shift, half):
        slot = SLOT[(shift, half)]
        for i in range(1 if shift == 2 else 4):
            arrived("ay", slot, i)
        mine = panel.at[slot, plane(k)]
        send(("sb", slot, 0), mine, mine, ak_s.at[slot, 0], ak_r.at[slot, 0], sibling)
        if (shift, half) in ((1, 0), (3, 1)):
            there = SLOT[(2, half)]
            send(("ay", there, 0), mine, panel.at[there, plane(k)], ay_s.at[there, 0], ay_r.at[there, 0],
                 at_y(4 - shift))

    every, first, second = slice(0, 2 * ff), slice(0, ff), slice(ff, 2 * ff)
    sign = (1, -1)

    def send_sum(u, way, s, cols, hops):
        send(("r", u, s, way), rs_out.at[u, way, s, :, cols], rs_in.at[u, way, s, :, cols], rs_s.at[u, way, s],
             rs_r.at[u, way, s], at_z(sign[way] * hops))

    def op_mm(u, part_no):
        shift, half = UNITS[u]
        cols = (first, second)[part_no]
        if part_no == 0:
            for i in range(1 if shift else 4):
                arrived("sb", u, i)
        load(part_no)
        part[u, :, cols] = jnp.dot(panel[u], wgu[:, cols], preferred_element_type=F32)
        far = 2 if SUMS[u] == "two" else 1
        rs_out[u, part_no, 0, :, cols] = part[u, chunk(4), cols].astype(BF)
        send_sum(u, part_no, 0, cols, far)
        if SUMS[u] == "two" and part_no == 1:
            for s, dist in ((1, 3), (3, 1)):
                for way in range(2):
                    rs_out[u, way, s] = part[u, chunk(sign[way] * dist), :].astype(BF)
                    send_sum(u, way, s, every, 1)

    def op_r(u, s, way):
        rows = chunk(sign[way] * (2 if SUMS[u] == "two" else 4 - s))
        got, rest = (first, second) if way == 0 else (second, first)
        arrived("r", u, s - 1, way)
        if SUMS[u] == "two":
            arrived("r", u, 1, way)
            rs_out[u, way, 2, :, got] = (part[u, rows, got] + rs_in[u, way, 1, :, got].astype(F32)
                                         + rs_in[u, way, 0, :, got].astype(F32)).astype(BF)
            rs_out[u, way, 2, :, rest] = (part[u, rows, rest] + rs_in[u, way, 1, :, rest].astype(F32)).astype(BF)
            send_sum(u, way, 2, every, 2)
        elif s == 3 and u in WIDE:
            i = WIDE.index(u)
            wide_out[i, way] = part[u, rows, :] + rs_in[u, way, 2].astype(F32)
            send(("r", u, s, way), wide_out.at[i, way], wide_in.at[i, way], rs_s.at[u, way, s], rs_r.at[u, way, s],
                 at_z(sign[way]))
        else:
            if s == 1:
                rs_out[u, way, s, :, got] = (part[u, rows, got] + rs_in[u, way, 0, :, got].astype(F32)).astype(BF)
                rs_out[u, way, s, :, rest] = part[u, rows, rest].astype(BF)
            else:
                rs_out[u, way, s] = (part[u, rows, :] + rs_in[u, way, s - 1].astype(F32)).astype(BF)
            send_sum(u, way, s, every, 1)

    def send_hidden(u, s, way, hops):
        behind = s if GATHERS[u] == "chain" else {0: 0, 1: 0, 2: 2, 3: 2}[s]
        piece = hid.at[u, chunk(-sign[way] * behind)]
        if s == 3:
            cols = slice(0, half_cut) if way == 0 else slice(half_cut, ff)
            piece = hid.at[u, chunk(-sign[way] * behind), cols]
        send(("a", u, s, way), piece, piece, ag_s.at[u, way, s], ag_r.at[u, way, s], at_z(sign[way] * hops))

    def op_g(u):
        rows = chunk(0)
        total = part[u, rows, :]
        for way in range(2):
            arrived("r", u, 3, way)
            if u in WIDE:
                total += wide_in[WIDE.index(u), way]
            else:
                total += rs_in[u, way, 3].astype(F32)
            if SUMS[u] == "two":
                arrived("r", u, 2, way)
                total += rs_in[u, way, 2].astype(F32)
        hid[u, rows, :] = (jax.nn.silu(total[:, :ff]) * total[:, ff:]).astype(BF)
        if GATHERS[u] == "two":
            for way in range(2):
                send_hidden(u, 1, way, 2)
        for way in range(2):
            send_hidden(u, 0, way, 1)

    def op_a(u, s, way):
        if GATHERS[u] == "two":
            arrived("a", u, 1, way)
            send_hidden(u, 2, way, 1)
            send_hidden(u, 3, way, 2)
        else:
            arrived("a", u, s - 1, way)
            send_hidden(u, s, way, 1)

    def op_pj(u):
        for way in range(2):
            if GATHERS[u] == "two":
                arrived("a", u, 0, way)
                arrived("a", u, 2, way)
            arrived("a", u, 3, way)
        load(2)

        @pl.loop(0, 2)
        def _(i):
            cols = pl.ds(pl.multiple_of(i * (width // 2), width // 2), width // 2)
            proj[u, :, cols] = jnp.dot(hid[u], wdn[:, cols], preferred_element_type=F32)

        send(("k", u), proj.at[u, plane(1 - k)], swap_in.at[u], k_s.at[u], k_r.at[u], sibling)

    def op_sc(u):
        arrived("k", u)
        for step in (2, 1, 3):
            there = lax.rem(x + step, 4)
            near = pl.ds(pl.multiple_of(there * ROWS, ROWS), ROWS)
            x_out[u, step - 1] = (proj[u, block(k, there), :] + swap_in[u, near, :]).astype(BF)
            send(("x", u, step), x_out.at[u, step - 1], x_in.at[u, step - 1], x_s.at[u, step - 1],
                 x_r.at[u, step - 1], at_x(step))

    def op_ty(u):
        shift, half = UNITS[u]
        near = pl.ds(pl.multiple_of(x * ROWS, ROWS), ROWS)
        total = proj[u, block(k, x), :] + swap_in[u, near, :]
        for step in (1, 3, 2):
            arrived("x", u, step)
            total += x_in[u, step - 1].astype(F32)
        if shift == 0:
            acc[pl.ds(half * ROWS, ROWS), :] = total
        else:
            y_out[shift - 1, half] = total
            send(("y", u), y_out.at[shift - 1, half], y_in.at[shift - 1, half], y_s.at[shift - 1, half],
                 y_r.at[shift - 1, half], at_y(shift))

    steps = {"x": op_x, "bx": op_bx, "by": op_by, "mm": op_mm, "r": op_r, "g": op_g, "a": op_a, "pj": op_pj,
             "sc": op_sc, "ty": op_ty}
    for step in ORDER:
        steps[step[0]](*step[1:])

    limit = jnp.where(c >= 4, lens[0, 1], lens[0, 0])
    for half in range(2):
        offset = lax.rem(c, 4) * (2 * ROWS) + half * ROWS + lax.broadcasted_iota(jnp.int32, (ROWS, 1), 0)
        keep = (offset < limit).astype(F32)
        total = acc[pl.ds(half * ROWS, ROWS), :]
        for shift in (1, 2, 3):
            arrived("y", SLOT[(shift, half)])
            total += y_in[shift - 1, half]
        out[pl.ds(half * ROWS, ROWS), :] = (total * keep).astype(BF)
    for copy in sent:
        copy.wait_send()


def local(activations, w_gate, w_up, w_down, seq_lengths):
    rows, depth = activations.shape
    ff = w_gate.shape[1]
    width = w_down.shape[1]
    dma = pltpu.SemaphoreType.DMA
    vmem = pl.BlockSpec(memory_space=pltpu.VMEM)
    hbm = pl.BlockSpec(memory_space=pl.ANY)
    return pl.pallas_call(
        kernel,
        out_shape=jax.ShapeDtypeStruct((rows, width), BF),
        in_specs=[vmem, hbm, hbm, hbm, pl.BlockSpec(memory_space=pltpu.SMEM)],
        out_specs=vmem,
        scratch_shapes=[
            pltpu.VMEM((N, UNIT, depth), BF),
            pltpu.VMEM((depth, 2 * ff), BF),
            pltpu.VMEM((ff, width), BF),
            pltpu.VMEM((N, UNIT, 2 * ff), F32),
            pltpu.VMEM((N, 2, 4, ROWS, 2 * ff), BF),
            pltpu.VMEM((N, 2, 4, ROWS, 2 * ff), BF),
            pltpu.VMEM((N_WIDE, 2, ROWS, 2 * ff), F32),
            pltpu.VMEM((N_WIDE, 2, ROWS, 2 * ff), F32),
            pltpu.VMEM((N, UNIT, ff), BF),
            pltpu.VMEM((N, UNIT, width), F32),
            pltpu.VMEM((N, UNIT // 2, width), F32),
            pltpu.VMEM((N, 3, ROWS, width), BF),
            pltpu.VMEM((N, 3, ROWS, width), BF),
            pltpu.VMEM((3, 2, ROWS, width), F32),
            pltpu.VMEM((3, 2, ROWS, width), F32),
            pltpu.VMEM((rows, width), F32),
            dma((3,)),
            dma((2, 3)), dma((2, 3)),
            dma((N, 4)), dma((N, 4)),
            dma((N, 4)), dma((N, 4)),
            dma((N, 2, 4)), dma((N, 2, 4)),
            dma((N, 2, 4)), dma((N, 2, 4)),
            dma((N,)), dma((N,)),
            dma((N, 3)), dma((N, 3)),
            dma((3, 2)), dma((3, 2)),
        ],
        compiler_params=pltpu.CompilerParams(collective_id=0, has_side_effects=True, vmem_limit_bytes=60 * 2**20),
        cost_estimate=pl.CostEstimate(flops=6 * 1024 * depth * ff, bytes_accessed=6 * depth * ff,
                                      transcendentals=128 * ff),
    )(activations, w_gate, w_up, w_down, seq_lengths)


def solution(mesh):
    return jax.shard_map(
        local,
        mesh=mesh,
        in_specs=(
            P(("dp", "col"), "row"),
            P("row", ("dp", "col")),
            P("row", ("dp", "col")),
            P(("dp", "col"), "row"),
            P("dp", None),
        ),
        out_specs=P(("dp", "col"), "row"),
        check_vma=False,
    )
```

```python
import jax
import jax.numpy as jnp
from jax import lax
from jax.experimental import pallas as pl
from jax.experimental.pallas import tpu as pltpu
from jax.sharding import PartitionSpec as P

MESH = pl.DeviceIdType.MESH
BF, F32 = jnp.bfloat16, jnp.float32
ROWS = 16
UNIT = 128
UNITS = [(0, 0), (3, 0), (2, 1), (1, 1), (1, 0), (0, 1), (3, 1), (2, 0)]
SUMS = ['two', 'chain', 'chainh', 'chainh', 'chainh', 'chain', 'chain', 'chainh']
GATHERS = ['chain', 'two', 'two', 'two', 'two', 'chain', 'chain', 'two']
X_WIDE = [0, 4]
SPLIT = [0, 1, 2, 3, 5, 6, 7]
ORDER = [
    ("x", 0), ("x", 1), ("bx", 0, 1), ("bx", 0, 3), ("bx", 0, 2), ("bx", 1, 1), ("mm", 0, 0), ("mm", 0, 1),
    ("bx", 1, 3), ("bx", 1, 2), ("mm", 5, 0), ("by", 1, 0), ("mm", 5, 1), ("by", 3, 0), ("mm", 4, 0),
    ("mm", 4, 1), ("r", 0, 1, 1), ("r", 0, 1, 0), ("mm", 1, 0), ("mm", 1, 1), ("r", 5, 1, 0), ("by", 1, 1),
    ("r", 5, 1, 1), ("by", 3, 1), ("r", 4, 1, 0), ("r", 4, 1, 1), ("mm", 3, 0), ("mm", 6, 0), ("mm", 3, 1),
    ("g", 0), ("mm", 6, 1), ("r", 5, 2, 0), ("r", 1, 1, 0), ("r", 5, 2, 1), ("by", 2, 0), ("r", 1, 1, 1),
    ("r", 4, 2, 0), ("r", 4, 2, 1), ("r", 3, 1, 0), ("mm", 7, 0), ("r", 6, 1, 0), ("r", 3, 1, 1), ("a", 0, 1, 0),
    ("a", 0, 1, 1), ("mm", 7, 1), ("by", 2, 1), ("r", 6, 1, 1), ("r", 5, 3, 0), ("r", 5, 3, 1), ("r", 1, 2, 0),
    ("mm", 2, 0), ("r", 1, 2, 1), ("mm", 2, 1), ("r", 4, 3, 1), ("r", 4, 3, 0), ("r", 3, 2, 0), ("r", 3, 2, 1),
    ("r", 7, 1, 0), ("a", 0, 2, 1), ("r", 7, 1, 1), ("r", 6, 2, 0), ("a", 0, 2, 0), ("r", 6, 2, 1), ("g", 5),
    ("r", 1, 3, 0), ("r", 1, 3, 1), ("r", 2, 1, 0), ("r", 2, 1, 1), ("g", 4), ("r", 3, 3, 0), ("r", 3, 3, 1),
    ("a", 0, 3, 1), ("r", 7, 2, 0), ("r", 7, 2, 1), ("r", 6, 3, 0), ("a", 0, 3, 0), ("r", 6, 3, 1),
    ("a", 5, 1, 0), ("a", 5, 1, 1), ("g", 1), ("r", 2, 2, 0), ("r", 2, 2, 1), ("a", 4, 2, 0), ("a", 4, 2, 1),
    ("g", 3), ("r", 7, 3, 0), ("r", 7, 3, 1), ("pj", 0, 0), ("g", 6), ("pj", 0, 1), ("a", 5, 2, 0),
    ("a", 5, 2, 1), ("sc", 0, 0), ("a", 1, 2, 0), ("a", 1, 2, 1), ("sc", 0, 1), ("r", 2, 3, 0), ("r", 2, 3, 1),
    ("pj", 4), ("a", 3, 2, 0), ("a", 3, 2, 1), ("ty", 0, 0), ("sc", 4), ("g", 7), ("a", 6, 1, 0), ("a", 6, 1, 1),
    ("a", 5, 3, 0), ("a", 5, 3, 1), ("ty", 0, 1), ("pj", 1, 0), ("pj", 1, 1), ("g", 2), ("sc", 1, 0),
    ("sc", 1, 1), ("pj", 3, 0), ("pj", 3, 1), ("a", 7, 2, 0), ("a", 7, 2, 1), ("a", 6, 2, 0), ("sc", 3, 0),
    ("a", 6, 2, 1), ("ty", 4), ("sc", 3, 1), ("pj", 5, 0), ("pj", 5, 1), ("a", 2, 2, 0), ("a", 2, 2, 1),
    ("ty", 1, 0), ("sc", 5, 0), ("ty", 1, 1), ("sc", 5, 1), ("a", 6, 3, 0), ("pj", 7, 0), ("a", 6, 3, 1),
    ("pj", 7, 1), ("ty", 3, 0), ("sc", 7, 0), ("ty", 3, 1), ("pj", 2, 0), ("sc", 7, 1), ("pj", 2, 1),
    ("pj", 6, 0), ("sc", 2, 0), ("ty", 5, 0), ("pj", 6, 1), ("ty", 5, 1), ("sc", 2, 1), ("sc", 6, 0),
    ("ty", 7, 0), ("sc", 6, 1), ("ty", 7, 1), ("ty", 2, 0), ("ty", 2, 1), ("ty", 6, 0), ("ty", 6, 1),
]
SLOT = {unit: i for i, unit in enumerate(UNITS)}
N = len(UNITS)
WIDE = [u for u in range(N) if SUMS[u] in ("chainf", "chainh")]
N_WIDE = max(1, len(WIDE))
N_X_WIDE = max(1, len(X_WIDE))


def kernel(act, w_gate, w_up, w_down, lens, out, panel, wgu, wdn, part, rs_out, rs_in, wide_out, wide_in, hid, proj,
           swap_in, x_out, x_in, xw_out, xw_in, y_out, y_in, acc, w_sem, ax_s, ax_r, ak_s, ak_r, ay_s, ay_r, rs_s, rs_r, wd_s, wd_r, ag_s,
           ag_r, k_s, k_r, x_s, x_r, y_s, y_r):
    y, z, c = lax.axis_index("dp"), lax.axis_index("row"), lax.axis_index("col")
    x, k = c // 2, lax.rem(c, 2)
    ff = w_gate.shape[1]
    width = w_down.shape[1]
    half_cut = 512

    def at_x(step):
        return (y, z, 2 * lax.rem(x + step, 4) + k)

    def at_y(step):
        return (lax.rem(y + step, 4), z, c)

    def at_z(step):
        return (y, lax.rem(z + step + 8, 8), c)

    sibling = (y, z, 2 * x + 1 - k)
    peers = [at_x(1), at_x(2), at_x(3), at_y(1), at_y(2), at_y(3), at_z(1), at_z(-1), at_z(2), at_z(-2), sibling]
    sent, live = [], {}

    def send(name, src, dst, ss, rs, device):
        copy = pltpu.make_async_remote_copy(src_ref=src, dst_ref=dst, send_sem=ss, recv_sem=rs, device_id=device,
                                            device_id_type=MESH)
        copy.start()
        sent.append(copy)
        live[name] = copy

    def arrived(*name):
        live.pop(name).wait_recv()

    weights = [
        pltpu.make_async_copy(w_gate, wgu.at[:, 0:ff], w_sem.at[0]),
        pltpu.make_async_copy(w_up, wgu.at[:, ff:2 * ff], w_sem.at[1]),
        pltpu.make_async_copy(w_down, wdn, w_sem.at[2]),
    ]
    barrier = pltpu.get_barrier_semaphore()
    for peer in peers:
        pl.semaphore_signal(barrier, inc=1, device_id=peer, device_id_type=MESH)
    for copy in weights:
        copy.start()
    pl.semaphore_wait(barrier, len(peers))
    loaded = set()

    def load(i):
        if i not in loaded:
            loaded.add(i)
            weights[i].wait()

    def block(plane, place):
        return pl.ds(pl.multiple_of((plane * 4 + place) * ROWS, ROWS), ROWS)

    def plane(which):
        return pl.ds(pl.multiple_of(which * 4 * ROWS, 4 * ROWS), 4 * ROWS)

    def chunk(step):
        return pl.ds(pl.multiple_of(lax.rem(z + step + 8, 8) * ROWS, ROWS), ROWS)

    def to_column(half, i, src):
        place = lax.rem(x + 4 - i, 4)
        slot = SLOT[(0, half)]
        send(("sb", slot, i), src, panel.at[slot, block(k, place)], ak_s.at[slot, i], ak_r.at[slot, i], sibling)
        for step in (1, 3):
            there = SLOT[(4 - step, half)]
            send(("ay", there, i), src, panel.at[there, block(k, place)], ay_s.at[there, i], ay_r.at[there, i],
                 at_y(step))

    def op_x(half):
        rows = pl.ds(half * ROWS, ROWS)
        slot = SLOT[(0, half)]
        for step in (1, 3, 2):
            send(("ax", half, step), act.at[rows], panel.at[slot, block(k, x)], ax_s.at[half, step - 1],
                 ax_r.at[half, step - 1], at_x(step))
        to_column(half, 0, act.at[rows])
        panel[slot, block(k, x), :] = act[rows, :]

    def op_bx(half, i):
        arrived("ax", half, i)
        to_column(half, i, panel.at[SLOT[(0, half)], block(k, lax.rem(x + 4 - i, 4))])

    def op_by(shift, half):
        slot = SLOT[(shift, half)]
        for i in range(1 if shift == 2 else 4):
            arrived("ay", slot, i)
        mine = panel.at[slot, plane(k)]
        send(("sb", slot, 0), mine, mine, ak_s.at[slot, 0], ak_r.at[slot, 0], sibling)
        if (shift, half) in ((1, 0), (3, 1)):
            there = SLOT[(2, half)]
            send(("ay", there, 0), mine, panel.at[there, plane(k)], ay_s.at[there, 0], ay_r.at[there, 0],
                 at_y(4 - shift))

    every, first, second = slice(0, 2 * ff), slice(0, ff), slice(ff, 2 * ff)
    sign = (1, -1)

    def send_sum(u, way, s, cols, hops):
        send(("r", u, s, way), rs_out.at[u, way, s, :, cols], rs_in.at[u, way, s, :, cols], rs_s.at[u, way, s],
             rs_r.at[u, way, s], at_z(sign[way] * hops))

    def op_mm(u, part_no):
        shift, half = UNITS[u]
        cols = (first, second)[part_no]
        if part_no == 0:
            for i in range(1 if shift else 4):
                arrived("sb", u, i)
        load(part_no)
        part[u, :, cols] = jnp.dot(panel[u], wgu[:, cols], preferred_element_type=F32)
        far = 2 if SUMS[u] == "two" else 1
        rs_out[u, part_no, 0, :, cols] = part[u, chunk(4), cols].astype(BF)
        send_sum(u, part_no, 0, cols, far)
        if SUMS[u] == "two" and part_no == 1:
            for s, dist in ((1, 3), (3, 1)):
                for way in range(2):
                    rs_out[u, way, s] = part[u, chunk(sign[way] * dist), :].astype(BF)
                    send_sum(u, way, s, every, 1)

    def op_r(u, s, way):
        rows = chunk(sign[way] * (2 if SUMS[u] == "two" else 4 - s))
        got, rest = (first, second) if way == 0 else (second, first)
        arrived("r", u, s - 1, way)
        if SUMS[u] == "two":
            arrived("r", u, 1, way)
            rs_out[u, way, 2, :, got] = (part[u, rows, got] + rs_in[u, way, 1, :, got].astype(F32)
                                         + rs_in[u, way, 0, :, got].astype(F32)).astype(BF)
            rs_out[u, way, 2, :, rest] = (part[u, rows, rest] + rs_in[u, way, 1, :, rest].astype(F32)).astype(BF)
            send_sum(u, way, 2, every, 2)
        elif s == 3 and u in WIDE:
            i = WIDE.index(u)
            cols = every if SUMS[u] == "chainf" else got
            wide_out[i, way, :, cols] = part[u, rows, cols] + rs_in[u, way, 2, :, cols].astype(F32)
            send(("w", u, way), wide_out.at[i, way, :, cols], wide_in.at[i, way, :, cols], wd_s.at[i, way],
                 wd_r.at[i, way], at_z(sign[way]))
            if SUMS[u] == "chainh":
                rs_out[u, way, s, :, rest] = (part[u, rows, rest] + rs_in[u, way, 2, :, rest].astype(F32)).astype(BF)
                send_sum(u, way, s, rest, 1)
        else:
            if s == 1:
                rs_out[u, way, s, :, got] = (part[u, rows, got] + rs_in[u, way, 0, :, got].astype(F32)).astype(BF)
                rs_out[u, way, s, :, rest] = part[u, rows, rest].astype(BF)
            else:
                rs_out[u, way, s] = (part[u, rows, :] + rs_in[u, way, s - 1].astype(F32)).astype(BF)
            send_sum(u, way, s, every, 1)

    def send_hidden(u, s, way, hops):
        behind = s if GATHERS[u] == "chain" else {0: 0, 1: 0, 2: 2, 3: 2}[s]
        piece = hid.at[u, chunk(-sign[way] * behind)]
        if s == 3:
            cols = slice(0, half_cut) if way == 0 else slice(half_cut, ff)
            piece = hid.at[u, chunk(-sign[way] * behind), cols]
        send(("a", u, s, way), piece, piece, ag_s.at[u, way, s], ag_r.at[u, way, s], at_z(sign[way] * hops))

    def op_g(u):
        rows = chunk(0)
        gate, up = part[u, rows, first], part[u, rows, second]
        for way in range(2):
            if u in WIDE:
                arrived("w", u, way)
            if SUMS[u] != "chainf":
                arrived("r", u, 3, way)
            if SUMS[u] == "two":
                arrived("r", u, 2, way)
                gate += rs_in[u, way, 2, :, first].astype(F32)
                up += rs_in[u, way, 2, :, second].astype(F32)
            wide_gate = u in WIDE and (SUMS[u] == "chainf" or way == 0)
            wide_up = u in WIDE and (SUMS[u] == "chainf" or way == 1)
            i = WIDE.index(u) if u in WIDE else 0
            gate += wide_in[i, way, :, first] if wide_gate else rs_in[u, way, 3, :, first].astype(F32)
            up += wide_in[i, way, :, second] if wide_up else rs_in[u, way, 3, :, second].astype(F32)
        hid[u, rows, :] = (jax.nn.silu(gate) * up).astype(BF)
        if GATHERS[u] == "two":
            for way in range(2):
                send_hidden(u, 1, way, 2)
        for way in range(2):
            send_hidden(u, 0, way, 1)

    def op_a(u, s, way):
        if GATHERS[u] == "two":
            arrived("a", u, 1, way)
            send_hidden(u, 2, way, 1)
            send_hidden(u, 3, way, 2)
        else:
            arrived("a", u, s - 1, way)
            send_hidden(u, s, way, 1)

    def part_cols(i):
        return slice(0, width) if i is None else slice(i * width // 2, (i + 1) * width // 2)

    def op_pj(u, i=None):
        if not i:
            for way in range(2):
                if GATHERS[u] == "two":
                    arrived("a", u, 0, way)
                    arrived("a", u, 2, way)
                arrived("a", u, 3, way)
        load(2)
        cols = part_cols(i)
        if i is None:
            @pl.loop(0, 2)
            def _(n):
                piece = pl.ds(pl.multiple_of(n * (width // 2), width // 2), width // 2)
                proj[u, :, piece] = jnp.dot(hid[u], wdn[:, piece], preferred_element_type=F32)
        else:
            proj[u, :, cols] = jnp.dot(hid[u], wdn[:, cols], preferred_element_type=F32)
        send(("k", u, i), proj.at[u, plane(1 - k), cols], swap_in.at[u, :, cols], k_s.at[u, i or 0],
             k_r.at[u, i or 0], sibling)

    def op_sc(u, i=None):
        arrived("k", u, i)
        cols = part_cols(i)
        for step in (2, 1, 3):
            there = lax.rem(x + step, 4)
            near = pl.ds(pl.multiple_of(there * ROWS, ROWS), ROWS)
            total = proj[u, block(k, there), cols] + swap_in[u, near, cols]
            if u in X_WIDE:
                w = X_WIDE.index(u)
                source, target = xw_out.at[w, step - 1, :, cols], xw_in.at[w, step - 1, :, cols]
                xw_out[w, step - 1, :, cols] = total
            else:
                source, target = x_out.at[u, step - 1, :, cols], x_in.at[u, step - 1, :, cols]
                x_out[u, step - 1, :, cols] = total.astype(BF)
            send(("x", u, step, i), source, target, x_s.at[u, step - 1, i or 0], x_r.at[u, step - 1, i or 0],
                 at_x(step))

    def op_ty(u, i=None):
        shift, half = UNITS[u]
        cols = part_cols(i)
        near = pl.ds(pl.multiple_of(x * ROWS, ROWS), ROWS)
        total = proj[u, block(k, x), cols] + swap_in[u, near, cols]
        for step in (1, 3, 2):
            arrived("x", u, step, i)
            if u in X_WIDE:
                total += xw_in[X_WIDE.index(u), step - 1, :, cols]
            else:
                total += x_in[u, step - 1, :, cols].astype(F32)
        if shift == 0:
            acc[pl.ds(half * ROWS, ROWS), cols] = total
        else:
            y_out[shift - 1, half, :, cols] = total
            send(("y", u, i), y_out.at[shift - 1, half, :, cols], y_in.at[shift - 1, half, :, cols],
                 y_s.at[shift - 1, half, i or 0], y_r.at[shift - 1, half, i or 0], at_y(shift))

    steps = {"x": op_x, "bx": op_bx, "by": op_by, "mm": op_mm, "r": op_r, "g": op_g, "a": op_a, "pj": op_pj,
             "sc": op_sc, "ty": op_ty}
    for step in ORDER:
        steps[step[0]](*step[1:])

    limit = jnp.where(c >= 4, lens[0, 1], lens[0, 0])
    for half in range(2):
        offset = lax.rem(c, 4) * (2 * ROWS) + half * ROWS + lax.broadcasted_iota(jnp.int32, (ROWS, 1), 0)
        keep = (offset < limit).astype(F32)
        total = acc[pl.ds(half * ROWS, ROWS), :]
        for shift in (1, 2, 3):
            u = SLOT[(shift, half)]
            for i in ((0, 1) if u in SPLIT else (None,)):
                arrived("y", u, i)
            total += y_in[shift - 1, half]
        out[pl.ds(half * ROWS, ROWS), :] = (total * keep).astype(BF)
    for copy in sent:
        copy.wait_send()


def local(activations, w_gate, w_up, w_down, seq_lengths):
    rows, depth = activations.shape
    ff = w_gate.shape[1]
    width = w_down.shape[1]
    dma = pltpu.SemaphoreType.DMA
    vmem = pl.BlockSpec(memory_space=pltpu.VMEM)
    hbm = pl.BlockSpec(memory_space=pl.ANY)
    return pl.pallas_call(
        kernel,
        out_shape=jax.ShapeDtypeStruct((rows, width), BF),
        in_specs=[vmem, hbm, hbm, hbm, pl.BlockSpec(memory_space=pltpu.SMEM)],
        out_specs=vmem,
        scratch_shapes=[
            pltpu.VMEM((N, UNIT, depth), BF),
            pltpu.VMEM((depth, 2 * ff), BF),
            pltpu.VMEM((ff, width), BF),
            pltpu.VMEM((N, UNIT, 2 * ff), F32),
            pltpu.VMEM((N, 2, 4, ROWS, 2 * ff), BF),
            pltpu.VMEM((N, 2, 4, ROWS, 2 * ff), BF),
            pltpu.VMEM((N_WIDE, 2, ROWS, 2 * ff), F32),
            pltpu.VMEM((N_WIDE, 2, ROWS, 2 * ff), F32),
            pltpu.VMEM((N, UNIT, ff), BF),
            pltpu.VMEM((N, UNIT, width), F32),
            pltpu.VMEM((N, UNIT // 2, width), F32),
            pltpu.VMEM((N, 3, ROWS, width), BF),
            pltpu.VMEM((N, 3, ROWS, width), BF),
            pltpu.VMEM((N_X_WIDE, 3, ROWS, width), F32),
            pltpu.VMEM((N_X_WIDE, 3, ROWS, width), F32),
            pltpu.VMEM((3, 2, ROWS, width), F32),
            pltpu.VMEM((3, 2, ROWS, width), F32),
            pltpu.VMEM((rows, width), F32),
            dma((3,)),
            dma((2, 3)), dma((2, 3)),
            dma((N, 4)), dma((N, 4)),
            dma((N, 4)), dma((N, 4)),
            dma((N, 2, 4)), dma((N, 2, 4)),
            dma((N_WIDE, 2)), dma((N_WIDE, 2)),
            dma((N, 2, 4)), dma((N, 2, 4)),
            dma((N, 2)), dma((N, 2)),
            dma((N, 3, 2)), dma((N, 3, 2)),
            dma((3, 2, 2)), dma((3, 2, 2)),
        ],
        compiler_params=pltpu.CompilerParams(collective_id=0, has_side_effects=True, vmem_limit_bytes=60 * 2**20),
        cost_estimate=pl.CostEstimate(flops=6 * 1024 * depth * ff, bytes_accessed=6 * depth * ff,
                                      transcendentals=128 * ff),
    )(activations, w_gate, w_up, w_down, seq_lengths)


def solution(mesh):
    return jax.shard_map(
        local,
        mesh=mesh,
        in_specs=(
            P(("dp", "col"), "row"),
            P("row", ("dp", "col")),
            P("row", ("dp", "col")),
            P(("dp", "col"), "row"),
            P("dp", None),
        ),
        out_specs=P(("dp", "col"), "row"),
        check_vma=False,
    )
```

```python
import jax
import jax.numpy as jnp
from jax import lax
from jax.experimental import pallas as pl
from jax.experimental.pallas import tpu as pltpu
from jax.sharding import PartitionSpec as P

MESH = pl.DeviceIdType.MESH
BF, F32 = jnp.bfloat16, jnp.float32
ROWS = 16
UNIT = 128
UNITS = [(0, 0), (1, 0), (3, 0), (2, 0), (1, 1), (2, 1), (3, 1), (0, 1)]
SUMS = ['two', 'chainh', 'chainh', 'chainh', 'chain', 'chain', 'chain', 'chain']
GATHERS = ['chain', 'chain', 'chain', 'chain', 'chain', 'chain', 'chain', 'chain']
X_WIDE = [0]
SPLIT = []
ORDER = [
    ("x", 0), ("x", 1), ("bx", 0, 1), ("bx", 0, 3), ("bx", 0, 2), ("bx", 1, 1), ("bx", 1, 3), ("mm", 0, 0),
    ("mm", 0, 1), ("bx", 1, 2), ("mm", 7, 0), ("by", 1, 0), ("by", 3, 0), ("mm", 7, 1), ("mm", 1, 0),
    ("mm", 1, 1), ("r", 0, 1, 1), ("r", 0, 1, 0), ("mm", 2, 0), ("mm", 2, 1), ("r", 1, 1, 0), ("r", 1, 1, 1),
    ("by", 1, 1), ("by", 3, 1), ("r", 7, 1, 0), ("r", 7, 1, 1), ("mm", 4, 0), ("r", 2, 1, 1), ("g", 0),
    ("r", 2, 1, 0), ("by", 2, 0), ("r", 1, 2, 1), ("r", 1, 2, 0), ("mm", 4, 1), ("mm", 3, 0), ("r", 2, 2, 1),
    ("a", 0, 1, 0), ("a", 0, 1, 1), ("r", 4, 1, 0), ("mm", 3, 1), ("r", 1, 3, 1), ("r", 2, 2, 0), ("r", 1, 3, 0),
    ("r", 4, 1, 1), ("r", 3, 1, 0), ("by", 2, 1), ("r", 2, 3, 1), ("a", 0, 2, 0), ("a", 0, 2, 1), ("mm", 6, 0),
    ("mm", 5, 0), ("r", 2, 3, 0), ("r", 3, 1, 1), ("r", 4, 2, 0), ("mm", 5, 1), ("r", 4, 2, 1), ("g", 1),
    ("mm", 6, 1), ("a", 0, 3, 0), ("r", 6, 1, 0), ("a", 0, 3, 1), ("r", 3, 2, 1), ("r", 5, 1, 0), ("r", 3, 2, 0),
    ("r", 7, 2, 1), ("g", 2), ("r", 4, 3, 1), ("r", 5, 1, 1), ("a", 1, 1, 1), ("r", 4, 3, 0), ("r", 6, 1, 1),
    ("a", 1, 1, 0), ("pj", 0), ("r", 3, 3, 1), ("r", 6, 2, 0), ("r", 7, 2, 0), ("r", 7, 3, 1), ("r", 5, 2, 0),
    ("a", 2, 1, 1), ("sc", 0), ("r", 3, 3, 0), ("a", 2, 1, 0), ("r", 5, 2, 1), ("g", 4), ("a", 1, 2, 1),
    ("a", 1, 2, 0), ("r", 6, 2, 1), ("r", 6, 3, 0), ("r", 7, 3, 0), ("ty", 0), ("r", 5, 3, 0), ("a", 2, 2, 1),
    ("g", 3), ("r", 5, 3, 1), ("a", 2, 2, 0), ("a", 4, 1, 1), ("a", 4, 1, 0), ("a", 1, 3, 1), ("a", 1, 3, 0),
    ("r", 6, 3, 1), ("a", 2, 3, 1), ("a", 3, 1, 1), ("g", 7), ("g", 5), ("a", 4, 2, 1), ("a", 3, 1, 0),
    ("a", 2, 3, 0), ("a", 4, 2, 0), ("g", 6), ("pj", 1), ("a", 5, 1, 0), ("a", 7, 1, 1), ("a", 3, 2, 1),
    ("a", 3, 2, 0), ("a", 5, 1, 1), ("pj", 2), ("a", 4, 3, 0), ("sc", 1), ("a", 4, 3, 1), ("a", 5, 2, 0),
    ("a", 7, 2, 1), ("a", 6, 1, 1), ("a", 6, 1, 0), ("a", 3, 3, 0), ("a", 3, 3, 1), ("sc", 2), ("a", 5, 2, 1),
    ("a", 7, 1, 0), ("pj", 4), ("a", 7, 3, 1), ("a", 5, 3, 0), ("a", 6, 2, 1), ("a", 6, 2, 0), ("pj", 3),
    ("a", 5, 3, 1), ("a", 7, 2, 0), ("sc", 4), ("ty", 1), ("a", 6, 3, 1), ("a", 6, 3, 0), ("sc", 3), ("pj", 5),
    ("a", 7, 3, 0), ("ty", 2), ("pj", 6), ("sc", 5), ("pj", 7), ("ty", 4), ("sc", 6), ("ty", 3), ("sc", 7),
    ("ty", 5), ("ty", 6), ("ty", 7),
]
SLOT = {unit: i for i, unit in enumerate(UNITS)}
N = len(UNITS)
WIDE = [u for u in range(N) if SUMS[u] in ("chainf", "chainh")]
N_WIDE = max(1, len(WIDE))
N_X_WIDE = max(1, len(X_WIDE))


def kernel(act, w_gate, w_up, w_down, lens, out, panel, wgu, wdn, part, rs_out, rs_in, wide_out, wide_in, hid, proj,
           swap_in, x_out, x_in, xw_out, xw_in, y_out, y_in, acc, w_sem, ax_s, ax_r, ak_s, ak_r, ay_s, ay_r, rs_s, rs_r, wd_s, wd_r, ag_s,
           ag_r, k_s, k_r, x_s, x_r, y_s, y_r):
    y, z, c = lax.axis_index("dp"), lax.axis_index("row"), lax.axis_index("col")
    x, k = c // 2, lax.rem(c, 2)
    ff = w_gate.shape[1]
    width = w_down.shape[1]
    half_cut = 512

    def at_x(step):
        return (y, z, 2 * lax.rem(x + step, 4) + k)

    def at_y(step):
        return (lax.rem(y + step, 4), z, c)

    def at_z(step):
        return (y, lax.rem(z + step + 8, 8), c)

    sibling = (y, z, 2 * x + 1 - k)
    peers = [at_x(1), at_x(2), at_x(3), at_y(1), at_y(2), at_y(3), at_z(1), at_z(-1), at_z(2), at_z(-2), sibling]
    sent, live = [], {}

    def send(name, src, dst, ss, rs, device):
        copy = pltpu.make_async_remote_copy(src_ref=src, dst_ref=dst, send_sem=ss, recv_sem=rs, device_id=device,
                                            device_id_type=MESH)
        copy.start()
        sent.append(copy)
        live[name] = copy

    def arrived(*name):
        live.pop(name).wait_recv()

    weights = [
        pltpu.make_async_copy(w_gate, wgu.at[:, 0:ff], w_sem.at[0]),
        pltpu.make_async_copy(w_up, wgu.at[:, ff:2 * ff], w_sem.at[1]),
        pltpu.make_async_copy(w_down, wdn, w_sem.at[2]),
    ]
    barrier = pltpu.get_barrier_semaphore()
    for peer in peers:
        pl.semaphore_signal(barrier, inc=1, device_id=peer, device_id_type=MESH)
    for copy in weights:
        copy.start()
    pl.semaphore_wait(barrier, len(peers))
    loaded = set()

    def load(i):
        if i not in loaded:
            loaded.add(i)
            weights[i].wait()

    def block(plane, place):
        return pl.ds(pl.multiple_of((plane * 4 + place) * ROWS, ROWS), ROWS)

    def plane(which):
        return pl.ds(pl.multiple_of(which * 4 * ROWS, 4 * ROWS), 4 * ROWS)

    def chunk(step):
        return pl.ds(pl.multiple_of(lax.rem(z + step + 8, 8) * ROWS, ROWS), ROWS)

    def to_column(half, i, src):
        place = lax.rem(x + 4 - i, 4)
        slot = SLOT[(0, half)]
        send(("sb", slot, i), src, panel.at[slot, block(k, place)], ak_s.at[slot, i], ak_r.at[slot, i], sibling)
        for step in (1, 3):
            there = SLOT[(4 - step, half)]
            send(("ay", there, i), src, panel.at[there, block(k, place)], ay_s.at[there, i], ay_r.at[there, i],
                 at_y(step))

    def op_x(half):
        rows = pl.ds(half * ROWS, ROWS)
        slot = SLOT[(0, half)]
        for step in (1, 3, 2):
            send(("ax", half, step), act.at[rows], panel.at[slot, block(k, x)], ax_s.at[half, step - 1],
                 ax_r.at[half, step - 1], at_x(step))
        to_column(half, 0, act.at[rows])
        panel[slot, block(k, x), :] = act[rows, :]

    def op_bx(half, i):
        arrived("ax", half, i)
        to_column(half, i, panel.at[SLOT[(0, half)], block(k, lax.rem(x + 4 - i, 4))])

    def op_by(shift, half):
        slot = SLOT[(shift, half)]
        for i in range(1 if shift == 2 else 4):
            arrived("ay", slot, i)
        mine = panel.at[slot, plane(k)]
        send(("sb", slot, 0), mine, mine, ak_s.at[slot, 0], ak_r.at[slot, 0], sibling)
        if (shift, half) in ((1, 0), (3, 1)):
            there = SLOT[(2, half)]
            send(("ay", there, 0), mine, panel.at[there, plane(k)], ay_s.at[there, 0], ay_r.at[there, 0],
                 at_y(4 - shift))

    every, first, second = slice(0, 2 * ff), slice(0, ff), slice(ff, 2 * ff)
    sign = (1, -1)

    def send_sum(u, way, s, cols, hops):
        send(("r", u, s, way), rs_out.at[u, way, s, :, cols], rs_in.at[u, way, s, :, cols], rs_s.at[u, way, s],
             rs_r.at[u, way, s], at_z(sign[way] * hops))

    def op_mm(u, part_no):
        shift, half = UNITS[u]
        cols = (first, second)[part_no]
        if part_no == 0:
            for i in range(1 if shift else 4):
                arrived("sb", u, i)
        load(part_no)
        part[u, :, cols] = jnp.dot(panel[u], wgu[:, cols], preferred_element_type=F32)
        far = 2 if SUMS[u] == "two" else 1
        rs_out[u, part_no, 0, :, cols] = part[u, chunk(4), cols].astype(BF)
        send_sum(u, part_no, 0, cols, far)
        if SUMS[u] == "two" and part_no == 1:
            for s, dist in ((1, 3), (3, 1)):
                for way in range(2):
                    rs_out[u, way, s] = part[u, chunk(sign[way] * dist), :].astype(BF)
                    send_sum(u, way, s, every, 1)

    def op_r(u, s, way):
        rows = chunk(sign[way] * (2 if SUMS[u] == "two" else 4 - s))
        got, rest = (first, second) if way == 0 else (second, first)
        arrived("r", u, s - 1, way)
        if SUMS[u] == "two":
            arrived("r", u, 1, way)
            rs_out[u, way, 2, :, got] = (part[u, rows, got] + rs_in[u, way, 1, :, got].astype(F32)
                                         + rs_in[u, way, 0, :, got].astype(F32)).astype(BF)
            rs_out[u, way, 2, :, rest] = (part[u, rows, rest] + rs_in[u, way, 1, :, rest].astype(F32)).astype(BF)
            send_sum(u, way, 2, every, 2)
        elif s == 3 and u in WIDE:
            i = WIDE.index(u)
            cols = every if SUMS[u] == "chainf" else got
            wide_out[i, way, :, cols] = part[u, rows, cols] + rs_in[u, way, 2, :, cols].astype(F32)
            send(("w", u, way), wide_out.at[i, way, :, cols], wide_in.at[i, way, :, cols], wd_s.at[i, way],
                 wd_r.at[i, way], at_z(sign[way]))
            if SUMS[u] == "chainh":
                rs_out[u, way, s, :, rest] = (part[u, rows, rest] + rs_in[u, way, 2, :, rest].astype(F32)).astype(BF)
                send_sum(u, way, s, rest, 1)
        else:
            if s == 1:
                rs_out[u, way, s, :, got] = (part[u, rows, got] + rs_in[u, way, 0, :, got].astype(F32)).astype(BF)
                rs_out[u, way, s, :, rest] = part[u, rows, rest].astype(BF)
            else:
                rs_out[u, way, s] = (part[u, rows, :] + rs_in[u, way, s - 1].astype(F32)).astype(BF)
            send_sum(u, way, s, every, 1)

    def send_hidden(u, s, way, hops):
        behind = s if GATHERS[u] == "chain" else {0: 0, 1: 0, 2: 2, 3: 2}[s]
        piece = hid.at[u, chunk(-sign[way] * behind)]
        if s == 3:
            cols = slice(0, half_cut) if way == 0 else slice(half_cut, ff)
            piece = hid.at[u, chunk(-sign[way] * behind), cols]
        send(("a", u, s, way), piece, piece, ag_s.at[u, way, s], ag_r.at[u, way, s], at_z(sign[way] * hops))

    def op_g(u):
        rows = chunk(0)
        gate, up = part[u, rows, first], part[u, rows, second]
        for way in range(2):
            if u in WIDE:
                arrived("w", u, way)
            if SUMS[u] != "chainf":
                arrived("r", u, 3, way)
            if SUMS[u] == "two":
                arrived("r", u, 2, way)
                gate += rs_in[u, way, 2, :, first].astype(F32)
                up += rs_in[u, way, 2, :, second].astype(F32)
            wide_gate = u in WIDE and (SUMS[u] == "chainf" or way == 0)
            wide_up = u in WIDE and (SUMS[u] == "chainf" or way == 1)
            i = WIDE.index(u) if u in WIDE else 0
            gate += wide_in[i, way, :, first] if wide_gate else rs_in[u, way, 3, :, first].astype(F32)
            up += wide_in[i, way, :, second] if wide_up else rs_in[u, way, 3, :, second].astype(F32)
        hid[u, rows, :] = (jax.nn.silu(gate) * up).astype(BF)
        if GATHERS[u] == "two":
            for way in range(2):
                send_hidden(u, 1, way, 2)
        for way in range(2):
            send_hidden(u, 0, way, 1)

    def op_a(u, s, way):
        if GATHERS[u] == "two":
            arrived("a", u, 1, way)
            send_hidden(u, 2, way, 1)
            send_hidden(u, 3, way, 2)
        else:
            arrived("a", u, s - 1, way)
            send_hidden(u, s, way, 1)

    def part_cols(i):
        return slice(0, width) if i is None else slice(i * width // 2, (i + 1) * width // 2)

    def op_pj(u, i=None):
        if not i:
            for way in range(2):
                if GATHERS[u] == "two":
                    arrived("a", u, 0, way)
                    arrived("a", u, 2, way)
                arrived("a", u, 3, way)
        load(2)
        cols = part_cols(i)
        if i is None:
            @pl.loop(0, 2)
            def _(n):
                piece = pl.ds(pl.multiple_of(n * (width // 2), width // 2), width // 2)
                proj[u, :, piece] = jnp.dot(hid[u], wdn[:, piece], preferred_element_type=F32)
        else:
            proj[u, :, cols] = jnp.dot(hid[u], wdn[:, cols], preferred_element_type=F32)
        send(("k", u, i), proj.at[u, plane(1 - k), cols], swap_in.at[u, :, cols], k_s.at[u, i or 0],
             k_r.at[u, i or 0], sibling)

    def op_sc(u, i=None):
        arrived("k", u, i)
        cols = part_cols(i)
        for step in (2, 1, 3):
            there = lax.rem(x + step, 4)
            near = pl.ds(pl.multiple_of(there * ROWS, ROWS), ROWS)
            total = proj[u, block(k, there), cols] + swap_in[u, near, cols]
            if u in X_WIDE:
                w = X_WIDE.index(u)
                source, target = xw_out.at[w, step - 1, :, cols], xw_in.at[w, step - 1, :, cols]
                xw_out[w, step - 1, :, cols] = total
            else:
                source, target = x_out.at[u, step - 1, :, cols], x_in.at[u, step - 1, :, cols]
                x_out[u, step - 1, :, cols] = total.astype(BF)
            send(("x", u, step, i), source, target, x_s.at[u, step - 1, i or 0], x_r.at[u, step - 1, i or 0],
                 at_x(step))

    def op_ty(u, i=None):
        shift, half = UNITS[u]
        cols = part_cols(i)
        near = pl.ds(pl.multiple_of(x * ROWS, ROWS), ROWS)
        total = proj[u, block(k, x), cols] + swap_in[u, near, cols]
        for step in (1, 3, 2):
            arrived("x", u, step, i)
            if u in X_WIDE:
                total += xw_in[X_WIDE.index(u), step - 1, :, cols]
            else:
                total += x_in[u, step - 1, :, cols].astype(F32)
        if shift == 0:
            acc[pl.ds(half * ROWS, ROWS), cols] = total
        else:
            y_out[shift - 1, half, :, cols] = total
            send(("y", u, i), y_out.at[shift - 1, half, :, cols], y_in.at[shift - 1, half, :, cols],
                 y_s.at[shift - 1, half, i or 0], y_r.at[shift - 1, half, i or 0], at_y(shift))

    steps = {"x": op_x, "bx": op_bx, "by": op_by, "mm": op_mm, "r": op_r, "g": op_g, "a": op_a, "pj": op_pj,
             "sc": op_sc, "ty": op_ty}
    for step in ORDER:
        steps[step[0]](*step[1:])

    limit = jnp.where(c >= 4, lens[0, 1], lens[0, 0])
    for half in range(2):
        offset = lax.rem(c, 4) * (2 * ROWS) + half * ROWS + lax.broadcasted_iota(jnp.int32, (ROWS, 1), 0)
        keep = (offset < limit).astype(F32)
        total = acc[pl.ds(half * ROWS, ROWS), :]
        for shift in (1, 2, 3):
            u = SLOT[(shift, half)]
            for i in ((0, 1) if u in SPLIT else (None,)):
                arrived("y", u, i)
            total += y_in[shift - 1, half]
        out[pl.ds(half * ROWS, ROWS), :] = (total * keep).astype(BF)
    for copy in sent:
        copy.wait_send()


def local(activations, w_gate, w_up, w_down, seq_lengths):
    rows, depth = activations.shape
    ff = w_gate.shape[1]
    width = w_down.shape[1]
    dma = pltpu.SemaphoreType.DMA
    vmem = pl.BlockSpec(memory_space=pltpu.VMEM)
    hbm = pl.BlockSpec(memory_space=pl.ANY)
    return pl.pallas_call(
        kernel,
        out_shape=jax.ShapeDtypeStruct((rows, width), BF),
        in_specs=[vmem, hbm, hbm, hbm, pl.BlockSpec(memory_space=pltpu.SMEM)],
        out_specs=vmem,
        scratch_shapes=[
            pltpu.VMEM((N, UNIT, depth), BF),
            pltpu.VMEM((depth, 2 * ff), BF),
            pltpu.VMEM((ff, width), BF),
            pltpu.VMEM((N, UNIT, 2 * ff), F32),
            pltpu.VMEM((N, 2, 4, ROWS, 2 * ff), BF),
            pltpu.VMEM((N, 2, 4, ROWS, 2 * ff), BF),
            pltpu.VMEM((N_WIDE, 2, ROWS, 2 * ff), F32),
            pltpu.VMEM((N_WIDE, 2, ROWS, 2 * ff), F32),
            pltpu.VMEM((N, UNIT, ff), BF),
            pltpu.VMEM((N, UNIT, width), F32),
            pltpu.VMEM((N, UNIT // 2, width), F32),
            pltpu.VMEM((N, 3, ROWS, width), BF),
            pltpu.VMEM((N, 3, ROWS, width), BF),
            pltpu.VMEM((N_X_WIDE, 3, ROWS, width), F32),
            pltpu.VMEM((N_X_WIDE, 3, ROWS, width), F32),
            pltpu.VMEM((3, 2, ROWS, width), F32),
            pltpu.VMEM((3, 2, ROWS, width), F32),
            pltpu.VMEM((rows, width), F32),
            dma((3,)),
            dma((2, 3)), dma((2, 3)),
            dma((N, 4)), dma((N, 4)),
            dma((N, 4)), dma((N, 4)),
            dma((N, 2, 4)), dma((N, 2, 4)),
            dma((N_WIDE, 2)), dma((N_WIDE, 2)),
            dma((N, 2, 4)), dma((N, 2, 4)),
            dma((N, 2)), dma((N, 2)),
            dma((N, 3, 2)), dma((N, 3, 2)),
            dma((3, 2, 2)), dma((3, 2, 2)),
        ],
        compiler_params=pltpu.CompilerParams(collective_id=0, has_side_effects=True, vmem_limit_bytes=60 * 2**20),
        cost_estimate=pl.CostEstimate(flops=6 * 1024 * depth * ff, bytes_accessed=6 * depth * ff,
                                      transcendentals=128 * ff),
    )(activations, w_gate, w_up, w_down, seq_lengths)


def solution(mesh):
    return jax.shard_map(
        local,
        mesh=mesh,
        in_specs=(
            P(("dp", "col"), "row"),
            P("row", ("dp", "col")),
            P("row", ("dp", "col")),
            P(("dp", "col"), "row"),
            P("dp", None),
        ),
        out_specs=P(("dp", "col"), "row"),
        check_vma=False,
    )
```
